32 devices in a mesh: groups: 2 (over x), slab: 16 (over z, y, core).
Axes of the slice: x: 2, y: 2, z: 4, core: 2. Of those that a mesh axis runs over, the one named last changes fastest.
Arguments:
- latent: bfloat16 [64, 32, 2048], P(None, ('groups', 'slab')), parts along dimension 1, may hold values from -6 to 6
- conv1_weight: bfloat16 [27, 64, 64], replicated, may hold values from -0.15625 to 0.15625
- conv2_weight: bfloat16 [27, 64, 64], replicated, may hold values from -0.15625 to 0.15625
- head: bfloat16 [64], replicated, may hold values from -2 to 2
- p_prev: float32 [32, 16, 64, 128], P(('groups', 'slab')), parts along dimension 0, may hold values from -6 to 6
- p_cur: float32 [32, 16, 64, 128], P(('groups', 'slab')), parts along dimension 0, may hold values from -6 to 6
- adjoint: bfloat16 [4, 32, 16, 64, 128], P(None, ('groups', 'slab')), parts along dimension 1, may hold values from -6 to 6
- wavelet: float32 [16, 4], P('groups'), parts along dimension 0, may hold values from -12 to 12
- sources: int32 [16, 3], P('groups'), parts along dimension 0, may hold values from 0 to 127, as said below
- receivers: int32 [16, 3, 128], P('groups'), parts along dimension 0, may hold values from 0 to 127, as said below
Outputs:
- pressure_final: float32 [32, 16, 64, 128], P(('groups', 'slab')), parts along dimension 0
- traces: float32 [16, 4, 128], P('groups'), parts along dimension 0
- gradient: float32 [32, 2048], P(('groups', 'slab')), parts along dimension 0
The draws below stay inside these ranges and needn't reach their ends.
There are 2 independent parts, one for each index of `groups`. The reference program is written for one: setup_inputs(seed, part) draws one part's arguments, and reference() takes and returns one part's arrays. A program takes and returns all parts, laid end to end along the dimension named above; an argument that names none is the same for every part. Nothing has to cross between parts.
Inputs may be any that keep to these rules, and one draw needn't show every extreme that they name: sources[s] is the source cell (depth, row, column) of shot s on the fine grid: depth below 32, row below 64, column below 128. receivers[s, :, k] is the cell (depth, row, column) of receiver k of shot s on the fine grid: depth below 32, row below 64, column below 128.
All inputs are finite; a program needn't handle non-finite values.
Results may differ from the reference program's by a relative error of at most 0.006.
Values may be sent and summed in bfloat16 or wider, within the bound.
A program may use at most 64 MiB of HBM per device.

```python
import jax
import jax.numpy as jnp
from jax import lax

CH = 64
CY = 32
CX = 64
SHOTS = 8
STEPS = 4
NREC = 128
SLABS = 2
NZC = 16
FZ = 32
FPS = 16
FY = 64
FX = 128
SLOTS = 16


def draw_sources(key, part):
    key_depth, key_row, key_col, key_pick = jax.random.split(jax.random.fold_in(key, 11), 4)
    depths = jax.random.randint(key_depth, (SHOTS,), 0, FZ)
    rows_drawn = jax.random.randint(key_row, (SHOTS,), 0, FY)
    cols_drawn = jax.random.randint(key_col, (SHOTS,), 0, FX)
    chosen = jax.random.randint(key_pick, (), 0, SHOTS)
    marked = jnp.arange(SHOTS) == chosen
    depths = jnp.where(marked, FZ - 1, depths)
    rows_drawn = jnp.where(marked, FY - 1, rows_drawn)
    cols_drawn = jnp.where(marked, FX - 1, cols_drawn)
    return jnp.stack([depths, rows_drawn, cols_drawn], axis=1).astype(jnp.int32)


def draw_receivers(key, part):
    key_depth, key_row, key_col, key_pick = jax.random.split(jax.random.fold_in(key, 23), 4)
    depths = jax.random.randint(key_depth, (SHOTS, NREC), 0, FZ)
    rows_drawn = jax.random.randint(key_row, (SHOTS, NREC), 0, FY)
    cols_drawn = jax.random.randint(key_col, (SHOTS, NREC), 0, FX)
    chosen = jax.random.randint(key_pick, (SHOTS, 1), 0, NREC)
    marked = jnp.arange(NREC)[None, :] == chosen
    depths = jnp.where(marked, FZ - 1, depths)
    rows_drawn = jnp.where(marked, FY - 1, rows_drawn)
    cols_drawn = jnp.where(marked, FX - 1, cols_drawn)
    return jnp.stack([depths, rows_drawn, cols_drawn], axis=1).astype(jnp.int32)


def block_levels(rng, shape, shards, smallest, top_value):
    def one(position, blocks):
        draws = jax.random.uniform(jax.random.fold_in(jax.random.fold_in(rng, 6), position), (blocks,), jnp.float32, smallest / len(shards), top_value / len(shards))
        return jnp.repeat(jnp.exp(draws), shape[position] // blocks).reshape((-1,) + (1,) * (len(shape) - position - 1))

    factor_of = one(*shards[0])
    for cut in shards[1:]:
        factor_of = factor_of * one(*cut)
    return factor_of


def scatter_about(rng, shape, width, bound, cuts=(), held_as=jnp.bfloat16):
    drawn = jax.random.normal(rng, shape, jnp.float32) * width
    if len(cuts) > 0:
        drawn = block_levels(rng, shape, cuts, -0.22, 0.18) * drawn
    return jnp.clip(drawn, min=-bound, max=bound).astype(held_as)


def setup_inputs(seed: int = 0, part: int = 0) -> dict:
    keys = jax.random.split(jax.random.key(seed), 11)
    own_keys = jax.random.split(jax.random.fold_in(keys[10], part), 11)
    latent = scatter_about(own_keys[0], (CH, NZC, CY * CX), 1.0, 6.0, ((1, 16),))
    conv1_weight = scatter_about(keys[1], (27, CH, CH), (27 * CH) ** -0.5, 0.15625)
    conv2_weight = scatter_about(keys[2], (27, CH, CH), (27 * CH) ** -0.5, 0.15625)
    head = scatter_about(keys[3], (CH,), (CH // 8) ** -0.5, 2.0)
    p_prev = scatter_about(own_keys[4], (SLOTS, FPS, FY, FX), 1.0, 6.0, ((0, 16),), jnp.float32)
    p_cur = scatter_about(own_keys[5], (SLOTS, FPS, FY, FX), 1.0, 6.0, ((0, 16),), jnp.float32)
    adjoint = scatter_about(own_keys[6], (STEPS, SLOTS, FPS, FY, FX), 1.0, 6.0, ((1, 16),))
    wavelet = scatter_about(own_keys[7], (SHOTS, STEPS), 3.0, 12.0, (), jnp.float32)
    sources = draw_sources(jax.random.fold_in(jax.random.fold_in(keys[10], part), 71), part)
    receivers = draw_receivers(jax.random.fold_in(jax.random.fold_in(keys[10], part), 71), part)
    return dict(latent=latent, conv1_weight=conv1_weight, conv2_weight=conv2_weight, head=head, p_prev=p_prev, p_cur=p_cur, adjoint=adjoint, wavelet=wavelet, sources=sources, receivers=receivers)


stencil_weights = (-205.0 / 72.0, 8.0 / 5.0, -1.0 / 5.0, 8.0 / 315.0, -1.0 / 560.0)
lowest_speed = 1.5
speed_range = 3.0
courant = 0.088
leak_slope = 0.2

def conv_layer(activation, weight):
    planes = activation.shape[1]
    cell_count = activation.shape[2]
    extended = jnp.pad(activation, ((0, 0), (1, 1), (CX + 1, CX + 1)))
    columns = jnp.arange(cell_count) % CX
    accumulated = jnp.zeros((weight.shape[1], planes, cell_count), jnp.float32)
    tap_index = 0
    for depth_off in range(3):
        for row_off in (-1, 0, 1):
            for col_off in (-1, 0, 1):
                begin_at = CX + 1 + row_off * CX + col_off
                piece = extended[:, depth_off:depth_off + planes, begin_at:begin_at + cell_count]
                column_valid = ((columns + col_off >= 0) & (columns + col_off < CX)).astype(jnp.float32)
                accumulated = accumulated + jnp.einsum('oi,izn->ozn', weight[tap_index], piece * column_valid, precision=lax.Precision.HIGHEST)
                tap_index += 1
    return accumulated

def double_axis(values, axis):
    length = values.shape[axis]
    lower_side = jnp.concatenate([lax.slice_in_dim(values, 0, 1, axis=axis), lax.slice_in_dim(values, 0, length - 1, axis=axis)], axis=axis)
    upper_side = jnp.concatenate([lax.slice_in_dim(values, 1, length, axis=axis), lax.slice_in_dim(values, length - 1, length, axis=axis)], axis=axis)
    even_part = 0.75 * values + 0.25 * lower_side
    odd_part = 0.75 * values + 0.25 * upper_side
    new_shape = list(values.shape)
    new_shape[axis] = 2 * length
    return jnp.stack([even_part, odd_part], axis=axis + 1).reshape(new_shape)

def upsample_whole(coarse):
    grid = coarse.reshape(coarse.shape[0], CY, CX)
    return double_axis(double_axis(double_axis(grid, 0), 1), 2)

def stencil(extended):
    depth_total = extended.shape[0] - 8
    row_total = extended.shape[1]
    col_total = extended.shape[2]
    padded = jnp.pad(extended, ((0, 0), (4, 4), (4, 4)))

    def window(depth_at, row_at, col_at):
        return padded[depth_at:depth_at + depth_total, row_at:row_at + row_total, col_at:col_at + col_total]
    accumulated = 3.0 * stencil_weights[0] * window(4, 4, 4)
    for reach in range(1, 5):
        near_sum = window(4 - reach, 4, 4) + window(4 + reach, 4, 4)
        near_sum = near_sum + window(4, 4 - reach, 4) + window(4, 4 + reach, 4)
        near_sum = near_sum + window(4, 4, 4 - reach) + window(4, 4, 4 + reach)
        accumulated = accumulated + stencil_weights[reach] * near_sum
    return accumulated

def propagate(prev_field, field, adjoint_shot, pulses, source, station, courant_sq):
    correlation = jnp.zeros(field.shape, jnp.float32)
    samples_list = []
    for step_index in range(STEPS):
        laplace_term = stencil(jnp.pad(field, ((4, 4), (0, 0), (0, 0))))
        correlation = correlation + adjoint_shot[step_index].astype(jnp.float32) * laplace_term
        advanced = 2.0 * field - prev_field + courant_sq * laplace_term
        advanced = advanced.at[source[0], source[1], source[2]].add(pulses[step_index])
        samples_list.append(advanced[station[0], station[1], station[2]])
        prev_field, field = (field, advanced)
    return (field, jnp.stack(samples_list), correlation)

def reference(latent, conv1_weight, conv2_weight, head, p_prev, p_cur, adjoint, wavelet, sources, receivers):
    hidden = jax.nn.leaky_relu(conv_layer(latent.astype(jnp.float32), conv1_weight.astype(jnp.float32)), leak_slope).astype(jnp.bfloat16)
    second = jax.nn.leaky_relu(conv_layer(hidden.astype(jnp.float32), conv2_weight.astype(jnp.float32)), leak_slope)
    logits = jnp.einsum('c,czn->zn', head.astype(jnp.float32), second, precision=lax.Precision.HIGHEST)
    speed = (lowest_speed + speed_range * jax.nn.sigmoid(logits)).astype(jnp.bfloat16)
    coarse_speed = speed.astype(jnp.float32)
    fine_speed = upsample_whole(coarse_speed)
    courant_sq = (courant * fine_speed) ** 2

    def to_shots(field):
        return field.reshape(SLABS, SHOTS, FPS, FY, FX).transpose(1, 0, 2, 3, 4).reshape(SHOTS, FZ, FY, FX)
    prev_shots = to_shots(p_prev)
    cur_shots = to_shots(p_cur)
    adjoint_shots = adjoint.reshape(STEPS, SLABS, SHOTS, FPS, FY, FX).transpose(2, 0, 1, 3, 4, 5).reshape(SHOTS, STEPS, FZ, FY, FX)

    def one_shot(carried, inputs):
        prev_field, field, adjoint_shot, pulses, source, station = inputs
        final_field, samples, correlation = propagate(prev_field, field, adjoint_shot, pulses, source, station, courant_sq)
        return (carried + correlation, (final_field, samples))
    start_sum = jnp.zeros((FZ, FY, FX), jnp.float32)
    summed, outputs = lax.scan(one_shot, start_sum, (prev_shots, cur_shots, adjoint_shots, wavelet, sources, receivers))
    final_fields, traces = outputs
    pressure_final = final_fields.reshape(SHOTS, SLABS, FPS, FY, FX).transpose(1, 0, 2, 3, 4).reshape(SLOTS, FPS, FY, FX)
    fine_gradient = 2.0 * courant * courant * fine_speed * summed
    unused, pullback = jax.vjp(upsample_whole, coarse_speed)
    gradient = pullback(fine_gradient)[0]
    return (pressure_final, traces, gradient)
```

```python
import functools

import jax
import jax.numpy as jnp
import numpy as np
from jax import lax
from jax.experimental import pallas as pl
from jax.experimental.pallas import tpu as pltpu
from jax.sharding import PartitionSpec as P

CY = 32
CX = 64
CELLS = CY * CX
CH = 64
SHOTS = 8
STEPS = 4
FPS = 16
FY = 64
FX = 128
PARTS = 4

C = (-205.0 / 72.0, 8.0 / 5.0, -1.0 / 5.0, 8.0 / 315.0, -1.0 / 560.0)
COURANT = 0.088
LEAK = 0.2
F32 = jnp.float32
BF16 = jnp.bfloat16


def banded(n):
    t = np.zeros((n, n), np.float64)
    for k in range(5):
        for i in range(n):
            for j in {i - k, i + k}:
                if 0 <= j < n:
                    t[i, j] = C[k]
    hi = t.astype(jnp.bfloat16).astype(np.float64)
    return hi, t - hi


def doubling(n):
    u = np.zeros((2 * n, n))
    for k in range(n):
        u[2 * k, k] += 0.75
        u[2 * k, max(k - 1, 0)] += 0.25
        u[2 * k + 1, k] += 0.75
        u[2 * k + 1, min(k + 1, n - 1)] += 0.25
    return u


def constants():
    hi, lo = banded(FX)
    along_x = np.concatenate([hi, hi, lo], axis=0)
    hi, lo = banded(FY)
    four = np.eye(4)
    along_y = np.concatenate([np.kron(four, hi), np.kron(four, hi), np.kron(four, lo)], axis=1)
    depth = np.zeros((FPS, SHOTS + 2))
    for k in range(SHOTS):
        depth[2 * k, k + 1] = 0.75
        depth[2 * k, k] = 0.25
        depth[2 * k + 1, k + 1] = 0.75
        depth[2 * k + 1, k + 2] = 0.25
    rows = doubling(CY)
    up_zy = np.concatenate([np.kron(depth, rows[:, 0::2]), np.kron(depth, rows[:, 1::2])], axis=1)
    up_x = np.kron(np.eye(2), doubling(CX).T)
    out = (along_x, along_y, up_zy, up_zy.T, up_x, up_x.T)
    return [jnp.asarray(a.astype(jnp.bfloat16)) for a in out]


def dot(a, b, dims=((1,), (0,))):
    return lax.dot_general(a, b, (dims, ((), ())), preferred_element_type=F32)


def two(v):
    hi = v.astype(BF16)
    return hi, (v - hi.astype(F32)).astype(BF16)


def kernel(
    n,
    latent,
    w1,
    w2,
    head,
    wavelet,
    sources,
    receivers,
    along_x,
    along_y,
    up_x,
    up_xt,
    prev_hbm,
    cur_hbm,
    adj_hbm,
    up_zy_hbm,
    up_zyt_hbm,
    final_out,
    traces_out,
    gradient_out,
    a1,
    a2,
    wp1,
    wp2,
    y,
    vel,
    vels,
    field,
    adj,
    up_zy,
    up_zyt,
    speed,
    corr,
    rim_out,
    rim_in,
    hot,
    rec,
    recs,
    gr,
    grs,
    total,
    local_sem,
    lat_s,
    lat_r,
    hid_s,
    hid_r,
    rim_s,
    rim_r,
    vel_s,
    vel_r,
    rec_s,
    rec_r,
    gr_s,
    gr_r,
):
    me = lax.axis_index("slab")
    shot = lax.rem(me, SHOTS)
    slab = me // SHOTS
    slabs = n // SHOTS
    has_low = slab > 0
    has_high = slab < slabs - 1
    steps_here = range(STEPS)

    inner = pl.ds(4, FPS)
    loads = [
        pltpu.make_async_copy(cur_hbm, field.at[1, inner], local_sem.at[0]),
        pltpu.make_async_copy(prev_hbm, field.at[0, inner], local_sem.at[1]),
        pltpu.make_async_copy(up_zy_hbm, up_zy, local_sem.at[2]),
        pltpu.make_async_copy(adj_hbm, adj, local_sem.at[3]),
        pltpu.make_async_copy(up_zyt_hbm, up_zyt, local_sem.at[4]),
    ]
    for load in loads:
        load.start()

    def remote(src, dst, send, recv, target):
        return pltpu.make_async_remote_copy(
            src_ref=src,
            dst_ref=dst,
            send_sem=send,
            recv_sem=recv,
            device_id={"slab": target},
            device_id_type=pl.DeviceIdType.MESH,
        )

    def peer(j):
        return lax.rem(me + j, n)

    barrier = pltpu.get_barrier_semaphore()

    def greet(j, carry):
        pl.semaphore_signal(
            barrier, inc=1, device_id={"slab": peer(j)}, device_id_type=pl.DeviceIdType.MESH
        )
        return carry

    lax.fori_loop(1, n, greet, 0)

    for a in (a1, a2):

        @pl.when(me == 0)
        def _():
            a[0] = jnp.zeros((CH, CELLS), BF16)

        @pl.when(me == n - 1)
        def _():
            a[2] = jnp.zeros((CH, CELLS), BF16)

    a1[1] = latent[...]
    pl.semaphore_wait(barrier, n - 1)

    width = CELLS // PARTS

    def lat_copy(side, part):
        cols = pl.ds(part * width, width)
        return remote(
            latent.at[:, cols],
            a1.at[2 * side, :, cols],
            lat_s.at[side, part],
            lat_r.at[side, part],
            peer(1 if side == 0 else n - 1),
        )

    height = CH // PARTS

    def hid_copy(side, part):
        rows = pl.ds(pl.multiple_of(part * height, height), height)
        return remote(
            a2.at[1, rows],
            a2.at[2 * side, rows],
            hid_s.at[side, part],
            hid_r.at[side, part],
            peer(1 if side == 0 else n - 1),
        )

    def rim_copy(side, step):
        return remote(
            rim_out.at[side, step],
            rim_in.at[side, step],
            rim_s.at[side, step],
            rim_r.at[side, step],
            peer(SHOTS if side == 0 else n - SHOTS),
        )

    sends = (me < n - 1, me > 0)
    gets = (me > 0, me < n - 1)
    rim_sends = (has_high, has_low)
    rim_gets = (has_low, has_high)

    for part in range(PARTS):
        for side in range(2):

            @pl.when(sends[side])
            def _():
                lat_copy(side, part).start()

    for w, packed in ((w1, wp1), (w2, wp2)):
        for tap in range(9):
            for dz in range(3):
                packed[tap * CH : (tap + 1) * CH, dz * CH : (dz + 1) * CH] = w[dz * 9 + tap]

    loads[0].wait()
    rim_out[0, 0] = field[1, FPS : FPS + 4].reshape(4 * FY, FX).astype(BF16)
    rim_out[1, 0] = field[1, 4:8].reshape(4 * FY, FX).astype(BF16)
    for side in range(2):

        @pl.when(rim_sends[side])
        def _():
            rim_copy(side, 0).start()

    @pl.when(jnp.logical_not(has_low))
    def _():
        field[:, 0:4] = jnp.zeros((2, 4, FY, FX), F32)

    @pl.when(jnp.logical_not(has_high))
    def _():
        field[:, FPS + 4 :] = jnp.zeros((2, 4, FY, FX), F32)

    corr[...] = jnp.zeros((FPS * FY, FX), F32)
    station = receivers[shot]
    station_row = (station[0:1] - slab * FPS) * FY + station[1:2]
    station_col = station[2:3]
    hot[...] = (
        (lax.broadcasted_iota(jnp.int32, (FPS * FY, FX), 0) == station_row)
        .astype(F32)
        .astype(BF16)
    )
    col_hot = (lax.broadcasted_iota(jnp.int32, (FX, FX), 0) == station_col).astype(F32)
    rec[...] = jnp.zeros((8, FX), F32)

    cell = lax.broadcasted_iota(jnp.int32, (1, CELLS), 1)
    col = lax.rem(cell, CX)
    keep_left = (col > 0).astype(F32)
    keep_right = (col < CX - 1).astype(F32)
    keep_up = (cell >= CX).astype(F32)
    keep_down = (cell < CELLS - CX).astype(F32)

    def multiply(packed, a, part):
        cols = slice(part * width, (part + 1) * width)
        block = jnp.concatenate([a[0, :, cols], a[1, :, cols], a[2, :, cols]], axis=0)
        y[:, :, cols] = dot(packed[...], block).reshape(9, CH, width)

    def gathered(first):
        sums = []
        for dx in range(3):
            above = y[dx, pl.ds(first, 8)]
            middle = y[3 + dx, pl.ds(first, 8)]
            below = y[6 + dx, pl.ds(first, 8)]
            sums.append(
                middle
                + keep_up * pltpu.roll(above, CX, 1)
                + keep_down * pltpu.roll(below, CELLS - CX, 1)
            )
        v = (
            sums[1]
            + keep_left * pltpu.roll(sums[0], 1, 1)
            + keep_right * pltpu.roll(sums[2], CELLS - 1, 1)
        )
        return jnp.where(v > 0, v, LEAK * v)

    for part in range(PARTS):
        for side in range(2):

            @pl.when(gets[side])
            def _():
                lat_copy(side, part).wait_recv()

        multiply(wp1, a1, part)

    def hidden_part(part, carry):
        first = pl.multiple_of(part * height, height)
        pieces = [gathered(pl.multiple_of(first + 8 * h, 8)) for h in range(height // 8)]
        a2[1, pl.ds(first, height)] = jnp.concatenate(pieces, axis=0).astype(BF16)
        for side in range(2):

            @pl.when(sends[side])
            def _():
                hid_copy(side, part).start()

        return carry

    lax.fori_loop(0, PARTS, hidden_part, 0)
    for part in range(PARTS):
        for side in range(2):

            @pl.when(gets[side])
            def _():
                hid_copy(side, part).wait_recv()

    for part in range(PARTS):
        multiply(wp2, a2, part)

    def logit_part(part, acc):
        first = pl.multiple_of(part * 8, 8)
        return acc + head[pl.ds(first, 8), 0:1] * gathered(first)

    logits = jnp.sum(
        lax.fori_loop(0, CH // 8, logit_part, jnp.zeros((8, CELLS), F32)), axis=0, keepdims=True
    )
    wave_speed = 1.5 + 3.0 / (1.0 + jnp.exp(-logits))
    rows16 = jnp.concatenate(
        [wave_speed[:, FX * j : FX * (j + 1)] for j in range(CELLS // FX)], axis=0
    )
    vel[...] = rows16.astype(BF16)

    def vel_copy(j):
        return remote(vel, vels.at[j], vel_s.at[j], vel_r.at[j], peer(j))

    def rec_copy(j):
        return remote(rec, recs.at[j], rec_s.at[j], rec_r.at[j], peer(j))

    def over_peers(what):
        def one(j, carry):
            what(j)
            return carry

        lax.fori_loop(1, n, one, 0)

    over_peers(lambda j: vel_copy(j).start())
    vels[0] = vel[...]
    over_peers(lambda j: vel_copy(j).wait_recv())

    planes = []
    for i in range(SHOTS + 2):
        plane = jnp.clip(slab * SHOTS - 1 + i, 0, n - 1)
        planes.append(vels[lax.rem(me - plane + n, n)])
    wide = dot(jnp.concatenate(planes, axis=0), up_x[...])
    tall = jnp.concatenate([wide[:, :FX], wide[:, FX:]], axis=0)
    hi, lo = two(tall)
    loads[2].wait()
    speed[...] = dot(up_zy[...], hi) + dot(up_zy[...], lo)

    loads[1].wait()
    loads[3].wait()
    source_at = (
        (sources[shot, 0] - slab * FPS) * (FY * FX) + sources[shot, 1] * FX + sources[shot, 2]
    )
    linear = lax.broadcasted_iota(jnp.int32, (4 * FY, FX), 0) * FX + lax.broadcasted_iota(
        jnp.int32, (4 * FY, FX), 1
    )

    def pair(t, cur, old, chunks):
        centres = [field[cur, 4 + 4 * c : 8 + 4 * c].reshape(4 * FY, FX) for c in chunks]
        halves = [two(v) for v in centres]
        across = jnp.concatenate(
            [jnp.concatenate([hi, lo, hi], axis=0) for hi, lo in halves], axis=1
        )
        from_rows = dot(along_y[...], across)
        for i, c in enumerate(chunks):
            v = centres[i]
            hi, lo = halves[i]
            lap = from_rows[:, FX * i : FX * (i + 1)]
            lap = lap + dot(jnp.concatenate([hi, lo, hi], axis=1), along_x[...])
            lap = lap + C[0] * v
            at = 4 + 4 * c
            for k in range(1, 5):
                near = field[cur, at - k : at - k + 4] + field[cur, at + k : at + k + 4]
                lap = lap + C[k] * near.reshape(4 * FY, FX)
            rows = slice(4 * FY * c, 4 * FY * (c + 1))
            courant = COURANT * speed[rows]
            pulse = jnp.where(linear == source_at - c * 4 * FY * FX, wavelet[shot, t], 0.0)
            before = field[old, at : at + 4].reshape(4 * FY, FX)
            new = 2.0 * v - before + courant * courant * lap + pulse
            corr[rows] += adj[t, 4 * c : 4 * c + 4].reshape(4 * FY, FX).astype(F32) * lap
            field[old, at : at + 4] = new.reshape(4, FY, FX)

    def step(t, carry):
        cur = lax.rem(t + 1, 2)
        old = lax.rem(t, 2)
        for side in range(2):

            @pl.when(rim_gets[side])
            def _():
                rim_copy(side, t).wait_recv()
                at = (FPS + 4) * side
                field[cur, at : at + 4] = rim_in[side, t].reshape(4, FY, FX).astype(F32)

        pair(t, cur, old, (0, 3))

        @pl.when(t < STEPS - 1)
        def _():
            rim_out[0, t + 1] = field[old, FPS : FPS + 4].reshape(4 * FY, FX).astype(BF16)
            rim_out[1, t + 1] = field[old, 4:8].reshape(4 * FY, FX).astype(BF16)
            for side in range(2):

                @pl.when(rim_sends[side])
                def _():
                    rim_copy(side, t + 1).start()

        pair(t, cur, old, (1, 2))
        hi, lo = two(field[old, 4 : 4 + FPS].reshape(FPS * FY, FX))
        seen = dot(hi, hot[...], ((0,), (0,))) + dot(lo, hot[...], ((0,), (0,)))
        seen = jnp.sum(seen * col_hot, axis=0, keepdims=True)
        rec[...] += jnp.where(lax.broadcasted_iota(jnp.int32, (8, FX), 0) == t, seen, 0.0)
        return carry

    lax.fori_loop(0, STEPS, step, 0)
    over_peers(lambda j: rec_copy(j).start())

    fine = (2.0 * COURANT * COURANT) * speed[...] * corr[...]
    hi, lo = two(fine)
    loads[4].wait()
    tall = dot(up_zyt[...], hi) + dot(up_zyt[...], lo)
    half = tall.shape[0] // 2
    hi, lo = two(jnp.concatenate([tall[:half], tall[half:]], axis=1))
    narrow = dot(hi, up_xt[...]) + dot(lo, up_xt[...])
    gr[...] = narrow.reshape(SHOTS + 2, 16, FX)

    @pl.when(jnp.logical_not(has_low))
    def _():
        gr[1] += gr[0]

    @pl.when(jnp.logical_not(has_high))
    def _():
        gr[SHOTS] += gr[SHOTS + 1]

    def gr_copy(j):
        other = lax.rem(shot + j, SHOTS)
        return remote(
            gr.at[other + 1], grs.at[j], gr_s.at[j], gr_r.at[j], slab * SHOTS + other
        )

    def low_copy(slot):
        return remote(
            gr.at[0], grs.at[slot], gr_s.at[8], gr_r.at[slot], lax.rem(slab * SHOTS - 1 + n, n)
        )

    def high_copy(slot):
        return remote(
            gr.at[SHOTS + 1],
            grs.at[slot],
            gr_s.at[9],
            gr_r.at[slot],
            lax.rem((slab + 1) * SHOTS, n),
        )

    @pl.when(has_low)
    def _():
        low_copy(8 + shot).start()

    @pl.when(has_high)
    def _():
        high_copy(16 + shot).start()

    for j in range(1, SHOTS):
        gr_copy(j).start()

    final_out[...] = field[(STEPS + 1) % 2, 4 : 4 + FPS]

    recs[0] = rec[...]
    over_peers(lambda j: rec_copy(j).wait_recv())
    for s in range(SHOTS):

        def slab_term(k, acc):
            return acc + recs[lax.rem(me - (k * SHOTS + s) + n, n)]

        summed = lax.fori_loop(0, slabs, slab_term, jnp.zeros((8, FX), F32))
        traces_out[s] = summed[:STEPS]

    total[...] = gr[shot + 1]
    for j in range(1, SHOTS):
        gr_copy(j).wait_recv()
        total[...] += grs[j]

    @pl.when((shot == SHOTS - 1) & has_high)
    def _():
        for s in range(SHOTS):
            low_copy(8 + s).wait_recv()
            total[...] += grs[8 + s]

    @pl.when((shot == 0) & has_low)
    def _():
        for s in range(SHOTS):
            high_copy(16 + s).wait_recv()
            total[...] += grs[16 + s]

    gradient_out[...] = total[...]

    for part in range(PARTS):
        for side in range(2):

            @pl.when(sends[side])
            def _():
                lat_copy(side, part).wait_send()
                hid_copy(side, part).wait_send()

    for t in steps_here:
        for side in range(2):

            @pl.when(rim_sends[side])
            def _():
                rim_copy(side, t).wait_send()

    over_peers(lambda j: vel_copy(j).wait_send())
    over_peers(lambda j: rec_copy(j).wait_send())
    for j in range(1, SHOTS):
        gr_copy(j).wait_send()

    @pl.when(has_low)
    def _():
        low_copy(8 + shot).wait_send()

    @pl.when(has_high)
    def _():
        high_copy(16 + shot).wait_send()


def body(
    n,
    latent,
    conv1_weight,
    conv2_weight,
    head,
    p_prev,
    p_cur,
    adjoint,
    wavelet,
    sources,
    receivers,
):
    along_x, along_y, up_zy, up_zyt, up_x, up_xt = constants()
    vmem = pl.BlockSpec(memory_space=pltpu.VMEM)
    smem = pl.BlockSpec(memory_space=pltpu.SMEM)
    hbm = pl.BlockSpec(memory_space=pl.ANY)
    dma = pltpu.SemaphoreType.DMA
    final, traces, gradient = pl.pallas_call(
        functools.partial(kernel, n),
        out_shape=(
            jax.ShapeDtypeStruct((FPS, FY, FX), F32),
            jax.ShapeDtypeStruct((SHOTS, STEPS, 128), F32),
            jax.ShapeDtypeStruct((16, FX), F32),
        ),
        in_specs=[vmem] * 4 + [smem] * 2 + [vmem] * 5 + [hbm] * 5,
        out_specs=(vmem, vmem, vmem),
        scratch_shapes=[
            pltpu.VMEM((3, CH, CELLS), BF16),
            pltpu.VMEM((3, CH, CELLS), BF16),
            pltpu.VMEM((9 * CH, 3 * CH), BF16),
            pltpu.VMEM((9 * CH, 3 * CH), BF16),
            pltpu.VMEM((9, CH, CELLS), F32),
            pltpu.VMEM((16, FX), BF16),
            pltpu.VMEM((n, 16, FX), BF16),
            pltpu.VMEM((2, FPS + 8, FY, FX), F32),
            pltpu.VMEM((STEPS, FPS, FY, FX), BF16),
            pltpu.VMEM(up_zy.shape, BF16),
            pltpu.VMEM(up_zyt.shape, BF16),
            pltpu.VMEM((FPS * FY, FX), F32),
            pltpu.VMEM((FPS * FY, FX), F32),
            pltpu.VMEM((2, STEPS, 4 * FY, FX), BF16),
            pltpu.VMEM((2, STEPS, 4 * FY, FX), BF16),
            pltpu.VMEM((FPS * FY, FX), BF16),
            pltpu.VMEM((8, FX), F32),
            pltpu.VMEM((n, 8, FX), F32),
            pltpu.VMEM((SHOTS + 2, 16, FX), F32),
            pltpu.VMEM((3 * SHOTS, 16, FX), F32),
            pltpu.VMEM((16, FX), F32),
            dma((5,)),
            dma((2, PARTS)),
            dma((2, PARTS)),
            dma((2, PARTS)),
            dma((2, PARTS)),
            dma((2, STEPS)),
            dma((2, STEPS)),
            dma((n,)),
            dma((n,)),
            dma((n,)),
            dma((n,)),
            dma((10,)),
            dma((3 * SHOTS,)),
        ],
        compiler_params=pltpu.CompilerParams(
            collective_id=0, has_side_effects=True, vmem_limit_bytes=48 * 2**20
        ),
    )(
        latent.reshape(CH, CELLS),
        conv1_weight,
        conv2_weight,
        jnp.broadcast_to(head.astype(F32)[:, None], (CH, 128)),
        wavelet,
        sources,
        receivers,
        along_x,
        along_y,
        up_x,
        up_xt,
        p_prev[0],
        p_cur[0],
        adjoint[:, 0],
        up_zy,
        up_zyt,
    )
    return final[None], traces, gradient.reshape(1, CELLS)


def solution(mesh):
    in_specs = (
        P(None, ("groups", "slab"), None),
        P(),
        P(),
        P(),
        P(("groups", "slab"), None, None, None),
        P(("groups", "slab"), None, None, None),
        P(None, ("groups", "slab"), None, None, None),
        P("groups", None),
        P("groups", None),
        P("groups", None, None),
    )
    out_specs = (
        P(("groups", "slab"), None, None, None),
        P("groups", None, None),
        P(("groups", "slab"), None),
    )
    return jax.shard_map(
        functools.partial(body, mesh.shape["slab"]),
        mesh=mesh,
        in_specs=in_specs,
        out_specs=out_specs,
        check_vma=False,
    )
```

```python
import functools

import jax
import jax.numpy as jnp
import numpy as np
from jax import lax
from jax.experimental import pallas as pl
from jax.experimental.pallas import tpu as pltpu
from jax.sharding import PartitionSpec as P

CY = 32
CX = 64
CELLS = CY * CX
CH = 64
SHOTS = 8
STEPS = 4
FPS = 16
FY = 64
FX = 128
VMEM_BYTES = 60 * 2**20
PARTS = 4

C = (-205.0 / 72.0, 8.0 / 5.0, -1.0 / 5.0, 8.0 / 315.0, -1.0 / 560.0)
COURANT = 0.088
LEAK = 0.2
F32 = jnp.float32
BF16 = jnp.bfloat16


def banded(n):
    t = np.zeros((n, n), np.float64)
    for k in range(5):
        for i in range(n):
            for j in {i - k, i + k}:
                if 0 <= j < n:
                    t[i, j] = C[k]
    hi = t.astype(jnp.bfloat16).astype(np.float64)
    return hi, t - hi


def doubling(n):
    u = np.zeros((2 * n, n))
    for k in range(n):
        u[2 * k, k] += 0.75
        u[2 * k, max(k - 1, 0)] += 0.25
        u[2 * k + 1, k] += 0.75
        u[2 * k + 1, min(k + 1, n - 1)] += 0.25
    return u


def constants():
    hi, lo = banded(FX)
    along_x = np.concatenate([hi, hi, lo], axis=0)
    hi, lo = banded(FY)
    four = np.eye(4)
    along_y = np.concatenate([np.kron(four, hi), np.kron(four, hi), np.kron(four, lo)], axis=1)
    depth = np.zeros((FPS, SHOTS + 2))
    for k in range(SHOTS):
        depth[2 * k, k + 1] = 0.75
        depth[2 * k, k] = 0.25
        depth[2 * k + 1, k + 1] = 0.75
        depth[2 * k + 1, k + 2] = 0.25
    rows = doubling(CY)
    up_zy = np.concatenate([np.kron(depth, rows[:, 0::2]), np.kron(depth, rows[:, 1::2])], axis=1)
    up_x = np.kron(np.eye(2), doubling(CX).T)
    out = (along_x, along_y, up_zy, up_zy.T, up_x, up_x.T)
    return [jnp.asarray(a.astype(jnp.bfloat16)) for a in out]


def dot(a, b, dims=((1,), (0,))):
    return lax.dot_general(a, b, (dims, ((), ())), preferred_element_type=F32)


def two(v):
    hi = v.astype(BF16)
    return hi, (v - hi.astype(F32)).astype(BF16)


def kernel(
    n,
    latent,
    w1_hbm,
    w2_hbm,
    head,
    wavelet_hbm,
    sources_hbm,
    receivers_hbm,
    along_x_hbm,
    along_y_hbm,
    up_x_hbm,
    up_xt_hbm,
    prev_hbm,
    cur_hbm,
    adj_hbm,
    up_zy_hbm,
    up_zyt_hbm,
    final_out,
    traces_out,
    gradient_out,
    w1,
    w2,
    wavelet,
    sources,
    receivers,
    along_x,
    along_y,
    up_x,
    up_xt,
    lap0,
    head_col,
    a1,
    a2,
    wp1,
    wp2,
    y,
    vel,
    vels,
    field,
    adj,
    up_zy,
    up_zyt,
    speed,
    corr,
    rim_out,
    rim_in,
    hot,
    rec,
    recs,
    gr,
    grs,
    total,
    local_sem,
    lat_s,
    lat_r,
    hid_s,
    hid_r,
    rim_s,
    rim_r,
    vel_s,
    vel_r,
    rec_s,
    rec_r,
    gr_s,
    gr_r,
):
    me = lax.axis_index("slab")
    shot = lax.rem(me, SHOTS)
    slab = me // SHOTS
    slabs = n // SHOTS
    has_low = slab > 0
    has_high = slab < slabs - 1

    inner = pl.ds(4, FPS)
    pairs = (
        (latent, a1.at[1]),
        (w1_hbm, w1),
        (cur_hbm, field.at[1, inner]),
        (w2_hbm, w2),
        (receivers_hbm, receivers),
        (along_y_hbm, along_y),
        (along_x_hbm, along_x),
        (adj_hbm, adj),
        (up_x_hbm, up_x),
        (up_zy_hbm, up_zy),
        (wavelet_hbm, wavelet),
        (sources_hbm, sources),
        (prev_hbm, field.at[0, inner]),
        (up_zyt_hbm, up_zyt),
        (up_xt_hbm, up_xt),
    )
    loads = [
        pltpu.make_async_copy(src, dst, local_sem.at[i]) for i, (src, dst) in enumerate(pairs)
    ]

    def remote(src, dst, send, recv, target):
        return pltpu.make_async_remote_copy(
            src_ref=src,
            dst_ref=dst,
            send_sem=send,
            recv_sem=recv,
            device_id={"slab": target},
            device_id_type=pl.DeviceIdType.MESH,
        )

    def peer(j):
        return lax.rem(me + j, n)

    barrier = pltpu.get_barrier_semaphore()

    def greet(j, carry):
        pl.semaphore_signal(
            barrier, inc=1, device_id={"slab": peer(j)}, device_id_type=pl.DeviceIdType.MESH
        )
        return carry

    lax.fori_loop(1, n, greet, 0)
    for load in loads:
        load.start()

    for a in (a1, a2):

        @pl.when(me == 0)
        def _():
            a[0] = jnp.zeros((CH, CELLS), BF16)

        @pl.when(me == n - 1)
        def _():
            a[2] = jnp.zeros((CH, CELLS), BF16)

    pl.semaphore_wait(barrier, n - 1)

    width = CELLS // PARTS

    def lat_copy(side, part):
        cols = pl.ds(part * width, width)
        return remote(
            latent.at[:, cols],
            a1.at[2 * side, :, cols],
            lat_s.at[side, part],
            lat_r.at[side, part],
            peer(1 if side == 0 else n - 1),
        )

    height = CH // PARTS

    def hid_copy(side, part):
        rows = pl.ds(pl.multiple_of(part * height, height), height)
        return remote(
            a2.at[1, rows],
            a2.at[2 * side, rows],
            hid_s.at[side, part],
            hid_r.at[side, part],
            peer(1 if side == 0 else n - 1),
        )

    def rim_copy(side, step):
        return remote(
            rim_out.at[side, step],
            rim_in.at[side, step],
            rim_s.at[side, step],
            rim_r.at[side, step],
            peer(SHOTS if side == 0 else n - SHOTS),
        )

    sends = (me < n - 1, me > 0)
    gets = (me > 0, me < n - 1)
    rim_sends = (has_high, has_low)
    rim_gets = (has_low, has_high)

    for part in range(PARTS):
        for side in range(2):

            @pl.when(sends[side])
            def _():
                lat_copy(side, part).start()

    loads[1].wait()
    loads[3].wait()
    for w, packed in ((w1, wp1), (w2, wp2)):
        for tap in range(9):
            for dz in range(3):
                packed[tap * CH : (tap + 1) * CH, dz * CH : (dz + 1) * CH] = w[dz * 9 + tap]

    loads[2].wait()
    rim_out[0, 0] = field[1, FPS : FPS + 4].reshape(4 * FY, FX).astype(BF16)
    rim_out[1, 0] = field[1, 4:8].reshape(4 * FY, FX).astype(BF16)
    for side in range(2):

        @pl.when(rim_sends[side])
        def _():
            rim_copy(side, 0).start()

    @pl.when(jnp.logical_not(has_low))
    def _():
        field[:, 0:4] = jnp.zeros((2, 4, FY, FX), F32)

    @pl.when(jnp.logical_not(has_high))
    def _():
        field[:, FPS + 4 :] = jnp.zeros((2, 4, FY, FX), F32)

    loads[4].wait()
    station = receivers[:, shot]
    station_row = (station[0:1] - slab * FPS) * FY + station[1:2]
    station_col = station[2:3]
    hot[...] = (
        (lax.broadcasted_iota(jnp.int32, (FPS * FY, FX), 0) == station_row)
        .astype(F32)
        .astype(BF16)
    )
    col_hot = (lax.broadcasted_iota(jnp.int32, (FX, FX), 0) == station_col).astype(F32)
    rec[...] = jnp.zeros((8, FX), F32)

    square = (CH, CH)
    diagonal = lax.broadcasted_iota(jnp.int32, square, 0) == lax.broadcasted_iota(
        jnp.int32, square, 1
    )
    spread = jnp.broadcast_to(head[...].astype(F32), square)
    head_col[...] = jnp.broadcast_to(
        jnp.sum(jnp.where(diagonal, spread, 0.0), axis=1, keepdims=True), (CH, 128)
    )

    cell = lax.broadcasted_iota(jnp.int32, (1, CELLS), 1)
    col = lax.rem(cell, CX)
    keep_left = (col > 0).astype(F32)
    keep_right = (col < CX - 1).astype(F32)
    keep_up = (cell >= CX).astype(F32)
    keep_down = (cell < CELLS - CX).astype(F32)

    def multiply(packed, a, part):
        cols = slice(part * width, (part + 1) * width)
        block = jnp.concatenate([a[0, :, cols], a[1, :, cols], a[2, :, cols]], axis=0)
        y[:, :, cols] = dot(packed[...], block).reshape(9, CH, width)

    def gathered(first):
        sums = []
        for dx in range(3):
            above = y[dx, pl.ds(first, 8)]
            middle = y[3 + dx, pl.ds(first, 8)]
            below = y[6 + dx, pl.ds(first, 8)]
            sums.append(
                middle
                + keep_up * pltpu.roll(above, CX, 1)
                + keep_down * pltpu.roll(below, CELLS - CX, 1)
            )
        v = (
            sums[1]
            + keep_left * pltpu.roll(sums[0], 1, 1)
            + keep_right * pltpu.roll(sums[2], CELLS - 1, 1)
        )
        return jnp.where(v > 0, v, LEAK * v)

    loads[0].wait()
    for part in range(PARTS):
        for side in range(2):

            @pl.when(gets[side])
            def _():
                lat_copy(side, part).wait_recv()

        multiply(wp1, a1, part)

    def hidden_part(part, carry):
        first = pl.multiple_of(part * height, height)
        pieces = [gathered(pl.multiple_of(first + 8 * h, 8)) for h in range(height // 8)]
        a2[1, pl.ds(first, height)] = jnp.concatenate(pieces, axis=0).astype(BF16)
        for side in range(2):

            @pl.when(sends[side])
            def _():
                hid_copy(side, part).start()

        return carry

    lax.fori_loop(0, PARTS, hidden_part, 0)
    def laplace(cur, chunks):
        centres = [field[cur, 4 + 4 * c : 8 + 4 * c].reshape(4 * FY, FX) for c in chunks]
        halves = [two(v) for v in centres]
        across = jnp.concatenate(
            [jnp.concatenate([hi, lo, hi], axis=0) for hi, lo in halves], axis=1
        )
        from_rows = dot(along_y[...], across)
        laps = []
        for i, c in enumerate(chunks):
            hi, lo = halves[i]
            lap = from_rows[:, FX * i : FX * (i + 1)]
            lap = lap + dot(jnp.concatenate([hi, lo, hi], axis=1), along_x[...])
            lap = lap + C[0] * centres[i]
            at = 4 + 4 * c
            for k in range(1, 5):
                near = field[cur, at - k : at - k + 4] + field[cur, at + k : at + k + 4]
                lap = lap + C[k] * near.reshape(4 * FY, FX)
            laps.append(lap)
        return laps

    def advance(t, cur, old, c, lap):
        at = 4 + 4 * c
        courant = COURANT * speed[4 * FY * c : 4 * FY * (c + 1)]
        pulse = jnp.where(linear == source_at - c * 4 * FY * FX, wavelet[t, shot], 0.0)
        v = field[cur, at : at + 4].reshape(4 * FY, FX)
        before = field[old, at : at + 4].reshape(4 * FY, FX)
        new = 2.0 * v - before + courant * courant * lap + pulse
        field[old, at : at + 4] = new.reshape(4, FY, FX)

    def weighted(t, c, lap):
        return adj[t, 4 * c : 4 * c + 4].reshape(4 * FY, FX).astype(F32) * lap

    def take_rims(t, cur):
        for side in range(2):

            @pl.when(rim_gets[side])
            def _():
                rim_copy(side, t).wait_recv()
                at = (FPS + 4) * side
                field[cur, at : at + 4] = rim_in[side, t].reshape(4, FY, FX).astype(F32)

    def give_rims(t, old):
        rim_out[0, t + 1] = field[old, FPS : FPS + 4].reshape(4 * FY, FX).astype(BF16)
        rim_out[1, t + 1] = field[old, 4:8].reshape(4 * FY, FX).astype(BF16)
        for side in range(2):

            @pl.when(rim_sends[side])
            def _():
                rim_copy(side, t + 1).start()

    def record(t, old):
        hi, lo = two(field[old, 4 : 4 + FPS].reshape(FPS * FY, FX))
        seen = dot(hi, hot[...], ((0,), (0,))) + dot(lo, hot[...], ((0,), (0,)))
        seen = jnp.sum(seen * col_hot, axis=0, keepdims=True)
        rec[...] += jnp.where(lax.broadcasted_iota(jnp.int32, (8, FX), 0) == t, seen, 0.0)

    for i in (5, 6, 7, 8, 9, 10, 11, 12):
        loads[i].wait()
    source_at = (
        (sources[0, shot] - slab * FPS) * (FY * FX) + sources[1, shot] * FX + sources[2, shot]
    )
    linear = lax.broadcasted_iota(jnp.int32, (4 * FY, FX), 0) * FX + lax.broadcasted_iota(
        jnp.int32, (4 * FY, FX), 1
    )

    take_rims(0, 1)
    for chunks in ((0, 3), (1, 2)):
        for c, lap in zip(chunks, laplace(1, chunks)):
            rows = slice(4 * FY * c, 4 * FY * (c + 1))
            lap0[rows] = lap
            corr[rows] = weighted(0, c, lap)
    for part in range(PARTS):
        for side in range(2):

            @pl.when(gets[side])
            def _():
                hid_copy(side, part).wait_recv()

    for part in range(PARTS):
        multiply(wp2, a2, part)

    def logit_part(part, acc):
        first = pl.multiple_of(part * 8, 8)
        return acc + head_col[pl.ds(first, 8), 0:1] * gathered(first)

    logits = jnp.sum(
        lax.fori_loop(0, CH // 8, logit_part, jnp.zeros((8, CELLS), F32)), axis=0, keepdims=True
    )
    wave_speed = 1.5 + 3.0 / (1.0 + jnp.exp(-logits))
    rows16 = jnp.concatenate(
        [wave_speed[:, FX * j : FX * (j + 1)] for j in range(CELLS // FX)], axis=0
    )
    vel[...] = rows16.astype(BF16)

    def vel_copy(j):
        return remote(vel, vels.at[j], vel_s.at[j], vel_r.at[j], peer(j))

    def rec_copy(j):
        return remote(rec, recs.at[j], rec_s.at[j], rec_r.at[j], peer(j))

    def over_peers(what):
        def one(j, carry):
            what(j)
            return carry

        lax.fori_loop(1, n, one, 0)

    over_peers(lambda j: vel_copy(j).start())
    vels[0] = vel[...]
    over_peers(lambda j: vel_copy(j).wait_recv())

    planes = []
    for i in range(SHOTS + 2):
        plane = jnp.clip(slab * SHOTS - 1 + i, 0, n - 1)
        planes.append(vels[lax.rem(me - plane + n, n)])
    wide = dot(jnp.concatenate(planes, axis=0), up_x[...])
    tall = jnp.concatenate([wide[:, :FX], wide[:, FX:]], axis=0)
    hi, lo = two(tall)
    speed[...] = dot(up_zy[...], hi) + dot(up_zy[...], lo)

    def step(t, carry):
        cur = lax.rem(t + 1, 2)
        old = lax.rem(t, 2)
        take_rims(t, cur)
        for chunks in ((0, 3), (1, 2)):
            for c, lap in zip(chunks, laplace(cur, chunks)):
                advance(t, cur, old, c, lap)
                corr[4 * FY * c : 4 * FY * (c + 1)] += weighted(t, c, lap)
            if chunks[0] == 0:
                pl.when(t < STEPS - 1)(lambda: give_rims(t, old))
        record(t, old)
        return carry

    for chunks in ((0, 3), (1, 2)):
        for c in chunks:
            advance(0, 1, 0, c, lap0[4 * FY * c : 4 * FY * (c + 1)])
        if chunks[0] == 0:
            give_rims(0, 0)
    record(0, 0)
    lax.fori_loop(1, STEPS, step, 0)
    store = pltpu.make_async_copy(
        field.at[(STEPS + 1) % 2, inner], final_out, local_sem.at[len(pairs)]
    )
    store.start()
    over_peers(lambda j: rec_copy(j).start())

    fine = (2.0 * COURANT * COURANT) * speed[...] * corr[...]
    hi, lo = two(fine)
    loads[13].wait()
    loads[14].wait()
    tall = dot(up_zyt[...], hi) + dot(up_zyt[...], lo)
    half = tall.shape[0] // 2
    hi, lo = two(jnp.concatenate([tall[:half], tall[half:]], axis=1))
    narrow = dot(hi, up_xt[...]) + dot(lo, up_xt[...])
    gr[...] = narrow.reshape(SHOTS + 2, 16, FX)

    @pl.when(jnp.logical_not(has_low))
    def _():
        gr[1] += gr[0]

    @pl.when(jnp.logical_not(has_high))
    def _():
        gr[SHOTS] += gr[SHOTS + 1]

    def gr_copy(j):
        other = lax.rem(shot + j, SHOTS)
        return remote(
            gr.at[other + 1], grs.at[j], gr_s.at[j], gr_r.at[j], slab * SHOTS + other
        )

    def low_copy(slot):
        return remote(
            gr.at[0], grs.at[slot], gr_s.at[8], gr_r.at[slot], lax.rem(slab * SHOTS - 1 + n, n)
        )

    def high_copy(slot):
        return remote(
            gr.at[SHOTS + 1],
            grs.at[slot],
            gr_s.at[9],
            gr_r.at[slot],
            lax.rem((slab + 1) * SHOTS, n),
        )

    @pl.when(has_low)
    def _():
        low_copy(8 + shot).start()

    @pl.when(has_high)
    def _():
        high_copy(16 + shot).start()

    for j in range(1, SHOTS):
        gr_copy(j).start()


    recs[0] = rec[...]
    over_peers(lambda j: rec_copy(j).wait_recv())
    for s in range(SHOTS):

        def slab_term(k, acc):
            return acc + recs[lax.rem(me - (k * SHOTS + s) + n, n)]

        summed = lax.fori_loop(0, slabs, slab_term, jnp.zeros((8, FX), F32))
        traces_out[s] = summed[:STEPS]

    total[...] = gr[shot + 1]
    for j in range(1, SHOTS):
        gr_copy(j).wait_recv()
        total[...] += grs[j]

    @pl.when((shot == SHOTS - 1) & has_high)
    def _():
        for s in range(SHOTS):
            low_copy(8 + s).wait_recv()
            total[...] += grs[8 + s]

    @pl.when((shot == 0) & has_low)
    def _():
        for s in range(SHOTS):
            high_copy(16 + s).wait_recv()
            total[...] += grs[16 + s]

    gradient_out[...] = total[...]

    store.wait()
    for part in range(PARTS):
        for side in range(2):

            @pl.when(sends[side])
            def _():
                lat_copy(side, part).wait_send()
                hid_copy(side, part).wait_send()

    for t in range(STEPS):
        for side in range(2):

            @pl.when(rim_sends[side])
            def _():
                rim_copy(side, t).wait_send()

    over_peers(lambda j: vel_copy(j).wait_send())
    over_peers(lambda j: rec_copy(j).wait_send())
    for j in range(1, SHOTS):
        gr_copy(j).wait_send()

    @pl.when(has_low)
    def _():
        low_copy(8 + shot).wait_send()

    @pl.when(has_high)
    def _():
        high_copy(16 + shot).wait_send()


def body(
    n,
    latent,
    conv1_weight,
    conv2_weight,
    head,
    p_prev,
    p_cur,
    adjoint,
    wavelet,
    sources,
    receivers,
):
    along_x, along_y, up_zy, up_zyt, up_x, up_xt = constants()
    vmem = pl.BlockSpec(memory_space=pltpu.VMEM)
    hbm = pl.BlockSpec(memory_space=pl.ANY)
    dma = pltpu.SemaphoreType.DMA
    final, traces, gradient = pl.pallas_call(
        functools.partial(kernel, n),
        out_shape=(
            jax.ShapeDtypeStruct((FPS, FY, FX), F32),
            jax.ShapeDtypeStruct((SHOTS, STEPS, 128), F32),
            jax.ShapeDtypeStruct((16, FX), F32),
        ),
        in_specs=[hbm] * 3 + [vmem] + [hbm] * 12,
        out_specs=(hbm, vmem, vmem),
        scratch_shapes=[
            pltpu.VMEM(conv1_weight.shape, BF16),
            pltpu.VMEM(conv2_weight.shape, BF16),
            pltpu.SMEM((STEPS, SHOTS), F32),
            pltpu.SMEM((3, SHOTS), jnp.int32),
            pltpu.VMEM((3, SHOTS, 128), jnp.int32),
            pltpu.VMEM(along_x.shape, BF16),
            pltpu.VMEM(along_y.shape, BF16),
            pltpu.VMEM(up_x.shape, BF16),
            pltpu.VMEM(up_xt.shape, BF16),
            pltpu.VMEM((FPS * FY, FX), F32),
            pltpu.VMEM((CH, 128), F32),
            pltpu.VMEM((3, CH, CELLS), BF16),
            pltpu.VMEM((3, CH, CELLS), BF16),
            pltpu.VMEM((9 * CH, 3 * CH), BF16),
            pltpu.VMEM((9 * CH, 3 * CH), BF16),
            pltpu.VMEM((9, CH, CELLS), F32),
            pltpu.VMEM((16, FX), BF16),
            pltpu.VMEM((n, 16, FX), BF16),
            pltpu.VMEM((2, FPS + 8, FY, FX), F32),
            pltpu.VMEM((STEPS, FPS, FY, FX), BF16),
            pltpu.VMEM(up_zy.shape, BF16),
            pltpu.VMEM(up_zyt.shape, BF16),
            pltpu.VMEM((FPS * FY, FX), F32),
            pltpu.VMEM((FPS * FY, FX), F32),
            pltpu.VMEM((2, STEPS, 4 * FY, FX), BF16),
            pltpu.VMEM((2, STEPS, 4 * FY, FX), BF16),
            pltpu.VMEM((FPS * FY, FX), BF16),
            pltpu.VMEM((8, FX), F32),
            pltpu.VMEM((n, 8, FX), F32),
            pltpu.VMEM((SHOTS + 2, 16, FX), F32),
            pltpu.VMEM((3 * SHOTS, 16, FX), F32),
            pltpu.VMEM((16, FX), F32),
            dma((16,)),
            dma((2, PARTS)),
            dma((2, PARTS)),
            dma((2, PARTS)),
            dma((2, PARTS)),
            dma((2, STEPS)),
            dma((2, STEPS)),
            dma((n,)),
            dma((n,)),
            dma((n,)),
            dma((n,)),
            dma((10,)),
            dma((3 * SHOTS,)),
        ],
        compiler_params=pltpu.CompilerParams(
            collective_id=0, has_side_effects=True, vmem_limit_bytes=VMEM_BYTES
        ),
    )(
        latent.reshape(CH, CELLS),
        conv1_weight,
        conv2_weight,
        head.reshape(1, CH),
        wavelet.T,
        sources.T,
        receivers.transpose(1, 0, 2),
        along_x,
        along_y,
        up_x,
        up_xt,
        p_prev[0],
        p_cur[0],
        adjoint[:, 0],
        up_zy,
        up_zyt,
    )
    return final[None], traces, gradient.reshape(1, CELLS)


def solution(mesh):
    in_specs = (
        P(None, ("groups", "slab"), None),
        P(),
        P(),
        P(),
        P(("groups", "slab"), None, None, None),
        P(("groups", "slab"), None, None, None),
        P(None, ("groups", "slab"), None, None, None),
        P("groups", None),
        P("groups", None),
        P("groups", None, None),
    )
    out_specs = (
        P(("groups", "slab"), None, None, None),
        P("groups", None, None),
        P(("groups", "slab"), None),
    )
    return jax.shard_map(
        functools.partial(body, mesh.shape["slab"]),
        mesh=mesh,
        in_specs=in_specs,
        out_specs=out_specs,
        check_vma=False,
    )
```

```python
import functools

import jax
import jax.numpy as jnp
import numpy as np
from jax import lax
from jax.experimental import pallas as pl
from jax.experimental.pallas import tpu as pltpu
from jax.sharding import PartitionSpec as P

CY = 32
CX = 64
CELLS = CY * CX
CH = 64
SHOTS = 8
STEPS = 4
FPS = 16
FY = 64
FX = 128
VMEM_BYTES = 60 * 2**20
PARTS = 4

C = (-205.0 / 72.0, 8.0 / 5.0, -1.0 / 5.0, 8.0 / 315.0, -1.0 / 560.0)
COURANT = 0.088
LEAK = 0.2
F32 = jnp.float32
BF16 = jnp.bfloat16


def banded(n):
    t = np.zeros((n, n), np.float64)
    for k in range(5):
        for i in range(n):
            for j in {i - k, i + k}:
                if 0 <= j < n:
                    t[i, j] = C[k]
    hi = t.astype(jnp.bfloat16).astype(np.float64)
    return hi, t - hi


def doubling(n):
    u = np.zeros((2 * n, n))
    for k in range(n):
        u[2 * k, k] += 0.75
        u[2 * k, max(k - 1, 0)] += 0.25
        u[2 * k + 1, k] += 0.75
        u[2 * k + 1, min(k + 1, n - 1)] += 0.25
    return u


def constants():
    hi, lo = banded(FX)
    along_x = np.concatenate([hi, hi, lo], axis=0)
    hi, lo = banded(FY)
    four = np.eye(4)
    along_y = np.concatenate([np.kron(four, hi), np.kron(four, hi), np.kron(four, lo)], axis=1)
    depth = np.zeros((FPS, SHOTS + 2))
    for k in range(SHOTS):
        depth[2 * k, k + 1] = 0.75
        depth[2 * k, k] = 0.25
        depth[2 * k + 1, k + 1] = 0.75
        depth[2 * k + 1, k + 2] = 0.25
    rows = doubling(CY)
    up_zy = np.concatenate([np.kron(depth, rows[:, 0::2]), np.kron(depth, rows[:, 1::2])], axis=1)
    up_x = np.kron(np.eye(2), doubling(CX).T)
    out = (along_x, along_y, up_zy, up_zy.T, up_x, up_x.T)
    return [jnp.asarray(a.astype(jnp.bfloat16)) for a in out]


def dot(a, b, dims=((1,), (0,))):
    return lax.dot_general(a, b, (dims, ((), ())), preferred_element_type=F32)


def two(v):
    hi = v.astype(BF16)
    return hi, (v - hi.astype(F32)).astype(BF16)


def kernel(
    n,
    latent,
    w1_hbm,
    w2_hbm,
    head,
    wavelet_hbm,
    sources_hbm,
    receivers_hbm,
    along_x_hbm,
    along_y_hbm,
    up_x_hbm,
    up_xt_hbm,
    prev_hbm,
    cur_hbm,
    adj_hbm,
    up_zy_hbm,
    up_zyt_hbm,
    final_out,
    traces_out,
    gradient_out,
    w1,
    w2,
    wavelet,
    sources,
    receivers,
    along_x,
    along_y,
    up_x,
    up_xt,
    lap0,
    head_col,
    a1,
    a2,
    wp1,
    wp2,
    y,
    vel,
    vels,
    field,
    adj,
    up_zy,
    up_zyt,
    speed,
    corr,
    rim_out,
    rim_in,
    hot,
    rec,
    recs,
    gr,
    grs,
    total,
    local_sem,
    lat_s,
    lat_r,
    hid_s,
    hid_r,
    rim_s,
    rim_r,
    vel_s,
    vel_r,
    rec_s,
    rec_r,
    gr_s,
    gr_r,
):
    me = lax.axis_index("slab")
    shot = lax.rem(me, SHOTS)
    slab = me // SHOTS
    slabs = n // SHOTS
    has_low = slab > 0
    has_high = slab < slabs - 1

    inner = pl.ds(4, FPS)
    pairs = (
        (latent, a1.at[1]),
        (w1_hbm, w1),
        (cur_hbm, field.at[1, inner]),
        (w2_hbm, w2),
        (receivers_hbm, receivers),
        (along_y_hbm, along_y),
        (along_x_hbm, along_x),
        (adj_hbm, adj),
        (up_x_hbm, up_x),
        (up_zy_hbm, up_zy),
        (wavelet_hbm, wavelet),
        (sources_hbm, sources),
        (prev_hbm, field.at[0, inner]),
        (up_zyt_hbm, up_zyt),
        (up_xt_hbm, up_xt),
    )
    loads = [
        pltpu.make_async_copy(src, dst, local_sem.at[i]) for i, (src, dst) in enumerate(pairs)
    ]

    def remote(src, dst, send, recv, target):
        return pltpu.make_async_remote_copy(
            src_ref=src,
            dst_ref=dst,
            send_sem=send,
            recv_sem=recv,
            device_id={"slab": target},
            device_id_type=pl.DeviceIdType.MESH,
        )

    def peer(j):
        return lax.rem(me + j, n)

    barrier = pltpu.get_barrier_semaphore()

    def greet(j, carry):
        pl.semaphore_signal(
            barrier, inc=1, device_id={"slab": peer(j)}, device_id_type=pl.DeviceIdType.MESH
        )
        return carry

    lax.fori_loop(1, n, greet, 0)
    for load in loads:
        load.start()

    for a in (a1, a2):

        @pl.when(me == 0)
        def _():
            a[0] = jnp.zeros((CH, CELLS), BF16)

        @pl.when(me == n - 1)
        def _():
            a[2] = jnp.zeros((CH, CELLS), BF16)

    pl.semaphore_wait(barrier, n - 1)

    width = CELLS // PARTS

    def lat_copy(side, part):
        cols = pl.ds(part * width, width)
        return remote(
            latent.at[:, cols],
            a1.at[2 * side, :, cols],
            lat_s.at[side, part],
            lat_r.at[side, part],
            peer(1 if side == 0 else n - 1),
        )

    height = CH // PARTS

    def hid_copy(side, part):
        rows = pl.ds(pl.multiple_of(part * height, height), height)
        return remote(
            a2.at[1, rows],
            a2.at[2 * side, rows],
            hid_s.at[side, part],
            hid_r.at[side, part],
            peer(1 if side == 0 else n - 1),
        )

    def rim_copy(side, step):
        return remote(
            rim_out.at[side, step],
            rim_in.at[side, step],
            rim_s.at[side, step],
            rim_r.at[side, step],
            peer(SHOTS if side == 0 else n - SHOTS),
        )

    sends = (me < n - 1, me > 0)
    gets = (me > 0, me < n - 1)
    rim_sends = (has_high, has_low)
    rim_gets = (has_low, has_high)

    for part in range(PARTS):
        for side in range(2):

            @pl.when(sends[side])
            def _():
                lat_copy(side, part).start()

    loads[1].wait()
    loads[3].wait()
    for w, packed in ((w1, wp1), (w2, wp2)):
        for tap in range(9):
            for dz in range(3):
                packed[tap * CH : (tap + 1) * CH, dz * CH : (dz + 1) * CH] = w[dz * 9 + tap]

    loads[2].wait()
    rim_out[0, 0] = field[1, FPS : FPS + 4].reshape(4 * FY, FX).astype(BF16)
    rim_out[1, 0] = field[1, 4:8].reshape(4 * FY, FX).astype(BF16)
    @pl.when(jnp.logical_not(has_low))
    def _():
        field[:, 0:4] = jnp.zeros((2, 4, FY, FX), F32)

    @pl.when(jnp.logical_not(has_high))
    def _():
        field[:, FPS + 4 :] = jnp.zeros((2, 4, FY, FX), F32)

    loads[4].wait()
    station = receivers[:, shot]
    station_row = (station[0:1] - slab * FPS) * FY + station[1:2]
    station_col = station[2:3]
    hot[...] = (
        (lax.broadcasted_iota(jnp.int32, (FPS * FY, FX), 0) == station_row)
        .astype(F32)
        .astype(BF16)
    )
    col_hot = (lax.broadcasted_iota(jnp.int32, (FX, FX), 0) == station_col).astype(F32)
    rec[...] = jnp.zeros((8, FX), F32)

    square = (CH, CH)
    diagonal = lax.broadcasted_iota(jnp.int32, square, 0) == lax.broadcasted_iota(
        jnp.int32, square, 1
    )
    spread = jnp.broadcast_to(head[...].astype(F32), square)
    head_col[...] = jnp.broadcast_to(
        jnp.sum(jnp.where(diagonal, spread, 0.0), axis=1, keepdims=True), (CH, 128)
    )

    cell = lax.broadcasted_iota(jnp.int32, (1, CELLS), 1)
    col = lax.rem(cell, CX)
    keep_left = (col > 0).astype(F32)
    keep_right = (col < CX - 1).astype(F32)
    keep_up = (cell >= CX).astype(F32)
    keep_down = (cell < CELLS - CX).astype(F32)

    def multiply(packed, a, part):
        cols = slice(part * width, (part + 1) * width)
        block = jnp.concatenate([a[0, :, cols], a[1, :, cols], a[2, :, cols]], axis=0)
        y[:, :, cols] = dot(packed[...], block).reshape(9, CH, width)

    def gathered(first):
        sums = []
        for dx in range(3):
            above = y[dx, pl.ds(first, 8)]
            middle = y[3 + dx, pl.ds(first, 8)]
            below = y[6 + dx, pl.ds(first, 8)]
            sums.append(
                middle
                + keep_up * pltpu.roll(above, CX, 1)
                + keep_down * pltpu.roll(below, CELLS - CX, 1)
            )
        v = (
            sums[1]
            + keep_left * pltpu.roll(sums[0], 1, 1)
            + keep_right * pltpu.roll(sums[2], CELLS - 1, 1)
        )
        return jnp.where(v > 0, v, LEAK * v)

    loads[0].wait()
    for part in range(PARTS):
        for side in range(2):

            @pl.when(gets[side])
            def _():
                lat_copy(side, part).wait_recv()

        multiply(wp1, a1, part)

    for side in range(2):

        @pl.when(rim_sends[side])
        def _():
            rim_copy(side, 0).start()

    def hidden_part(part, carry):
        first = pl.multiple_of(part * height, height)
        pieces = [gathered(pl.multiple_of(first + 8 * h, 8)) for h in range(height // 8)]
        a2[1, pl.ds(first, height)] = jnp.concatenate(pieces, axis=0).astype(BF16)
        for side in range(2):

            @pl.when(sends[side])
            def _():
                hid_copy(side, part).start()

        return carry

    lax.fori_loop(0, PARTS, hidden_part, 0)
    def in_plane(cur, chunks):
        centres = [field[cur, 4 + 4 * c : 8 + 4 * c].reshape(4 * FY, FX) for c in chunks]
        halves = [two(v) for v in centres]
        across = jnp.concatenate(
            [jnp.concatenate([hi, lo, hi], axis=0) for hi, lo in halves], axis=1
        )
        from_rows = dot(along_y[...], across)
        laps = []
        for i, c in enumerate(chunks):
            hi, lo = halves[i]
            lap = from_rows[:, FX * i : FX * (i + 1)]
            lap = lap + dot(jnp.concatenate([hi, lo, hi], axis=1), along_x[...])
            laps.append(lap + C[0] * centres[i])
        return laps

    def in_depth(cur, chunks, laps):
        whole = []
        for c, lap in zip(chunks, laps):
            at = 4 + 4 * c
            for k in range(1, 5):
                near = field[cur, at - k : at - k + 4] + field[cur, at + k : at + k + 4]
                lap = lap + C[k] * near.reshape(4 * FY, FX)
            whole.append(lap)
        return whole

    def laplace(cur, chunks):
        return in_depth(cur, chunks, in_plane(cur, chunks))

    def advance(t, cur, old, c, lap):
        at = 4 + 4 * c
        courant = COURANT * speed[4 * FY * c : 4 * FY * (c + 1)]
        pulse = jnp.where(linear == source_at - c * 4 * FY * FX, wavelet[t, shot], 0.0)
        v = field[cur, at : at + 4].reshape(4 * FY, FX)
        before = field[old, at : at + 4].reshape(4 * FY, FX)
        new = 2.0 * v - before + courant * courant * lap + pulse
        field[old, at : at + 4] = new.reshape(4, FY, FX)

    def weighted(t, c, lap):
        return adj[t, 4 * c : 4 * c + 4].reshape(4 * FY, FX).astype(F32) * lap

    def take_rims(t, cur):
        for side in range(2):

            @pl.when(rim_gets[side])
            def _():
                rim_copy(side, t).wait_recv()
                at = (FPS + 4) * side
                field[cur, at : at + 4] = rim_in[side, t].reshape(4, FY, FX).astype(F32)

    def give_rims(t, old):
        rim_out[0, t + 1] = field[old, FPS : FPS + 4].reshape(4 * FY, FX).astype(BF16)
        rim_out[1, t + 1] = field[old, 4:8].reshape(4 * FY, FX).astype(BF16)
        for side in range(2):

            @pl.when(rim_sends[side])
            def _():
                rim_copy(side, t + 1).start()

    def record(t, old):
        hi, lo = two(field[old, 4 : 4 + FPS].reshape(FPS * FY, FX))
        seen = dot(hi, hot[...], ((0,), (0,))) + dot(lo, hot[...], ((0,), (0,)))
        seen = jnp.sum(seen * col_hot, axis=0, keepdims=True)
        rec[...] += jnp.where(lax.broadcasted_iota(jnp.int32, (8, FX), 0) == t, seen, 0.0)

    for i in (5, 6, 7, 8, 9, 10, 11, 12):
        loads[i].wait()
    source_at = (
        (sources[0, shot] - slab * FPS) * (FY * FX) + sources[1, shot] * FX + sources[2, shot]
    )
    linear = lax.broadcasted_iota(jnp.int32, (4 * FY, FX), 0) * FX + lax.broadcasted_iota(
        jnp.int32, (4 * FY, FX), 1
    )

    take_rims(0, 1)
    for chunks in ((0, 3), (1, 2)):
        for c, lap in zip(chunks, laplace(1, chunks)):
            rows = slice(4 * FY * c, 4 * FY * (c + 1))
            lap0[rows] = lap
            corr[rows] = weighted(0, c, lap)
    for part in range(PARTS):
        for side in range(2):

            @pl.when(gets[side])
            def _():
                hid_copy(side, part).wait_recv()

    for part in range(PARTS):
        multiply(wp2, a2, part)

    def logit_part(part, acc):
        first = pl.multiple_of(part * 8, 8)
        return acc + head_col[pl.ds(first, 8), 0:1] * gathered(first)

    logits = jnp.sum(
        lax.fori_loop(0, CH // 8, logit_part, jnp.zeros((8, CELLS), F32)), axis=0, keepdims=True
    )
    wave_speed = 1.5 + 3.0 / (1.0 + jnp.exp(-logits))
    rows16 = jnp.concatenate(
        [wave_speed[:, FX * j : FX * (j + 1)] for j in range(CELLS // FX)], axis=0
    )
    vel[...] = rows16.astype(BF16)

    def vel_copy(j):
        return remote(vel, vels.at[j], vel_s.at[j], vel_r.at[j], peer(j))

    def rec_copy(j):
        return remote(rec, recs.at[j], rec_s.at[j], rec_r.at[j], peer(j))

    def over_peers(what):
        def one(j, carry):
            what(j)
            return carry

        lax.fori_loop(1, n, one, 0)

    over_peers(lambda j: vel_copy(j).start())
    vels[0] = vel[...]
    over_peers(lambda j: vel_copy(j).wait_recv())

    planes = []
    for i in range(SHOTS + 2):
        plane = jnp.clip(slab * SHOTS - 1 + i, 0, n - 1)
        planes.append(vels[lax.rem(me - plane + n, n)])
    wide = dot(jnp.concatenate(planes, axis=0), up_x[...])
    tall = jnp.concatenate([wide[:, :FX], wide[:, FX:]], axis=0)
    hi, lo = two(tall)
    speed[...] = dot(up_zy[...], hi) + dot(up_zy[...], lo)

    def step(t, carry):
        cur = lax.rem(t + 1, 2)
        old = lax.rem(t, 2)
        outer, middle = (0, 3), (1, 2)
        laps = in_plane(cur, outer)
        take_rims(t, cur)
        laps = in_depth(cur, outer, laps)
        for c, lap in zip(outer, laps):
            advance(t, cur, old, c, lap)
        pl.when(t < STEPS - 1)(lambda: give_rims(t, old))
        laps = laps + laplace(cur, middle)
        for c, lap in zip(middle, laps[2:]):
            advance(t, cur, old, c, lap)
        for c, lap in zip(outer + middle, laps):
            corr[4 * FY * c : 4 * FY * (c + 1)] += weighted(t, c, lap)
        record(t, old)
        return carry

    for chunks in ((0, 3), (1, 2)):
        for c in chunks:
            advance(0, 1, 0, c, lap0[4 * FY * c : 4 * FY * (c + 1)])
        if chunks[0] == 0:
            give_rims(0, 0)
    record(0, 0)
    lax.fori_loop(1, STEPS, step, 0)
    store = pltpu.make_async_copy(
        field.at[(STEPS + 1) % 2, inner], final_out, local_sem.at[len(pairs)]
    )
    store.start()
    over_peers(lambda j: rec_copy(j).start())

    fine = (2.0 * COURANT * COURANT) * speed[...] * corr[...]
    hi, lo = two(fine)
    loads[13].wait()
    loads[14].wait()
    tall = dot(up_zyt[...], hi) + dot(up_zyt[...], lo)
    half = tall.shape[0] // 2
    hi, lo = two(jnp.concatenate([tall[:half], tall[half:]], axis=1))
    narrow = dot(hi, up_xt[...]) + dot(lo, up_xt[...])
    gr[...] = narrow.reshape(SHOTS + 2, 16, FX)

    @pl.when(jnp.logical_not(has_low))
    def _():
        gr[1] += gr[0]

    @pl.when(jnp.logical_not(has_high))
    def _():
        gr[SHOTS] += gr[SHOTS + 1]

    def gr_copy(j):
        other = lax.rem(shot + j, SHOTS)
        return remote(
            gr.at[other + 1], grs.at[j], gr_s.at[j], gr_r.at[j], slab * SHOTS + other
        )

    def low_copy(slot):
        return remote(
            gr.at[0], grs.at[slot], gr_s.at[8], gr_r.at[slot], lax.rem(slab * SHOTS - 1 + n, n)
        )

    def high_copy(slot):
        return remote(
            gr.at[SHOTS + 1],
            grs.at[slot],
            gr_s.at[9],
            gr_r.at[slot],
            lax.rem((slab + 1) * SHOTS, n),
        )

    @pl.when(has_low)
    def _():
        low_copy(8 + shot).start()

    @pl.when(has_high)
    def _():
        high_copy(16 + shot).start()

    for j in range(1, SHOTS):
        gr_copy(j).start()


    recs[0] = rec[...]
    over_peers(lambda j: rec_copy(j).wait_recv())
    for s in range(SHOTS):

        def slab_term(k, acc):
            return acc + recs[lax.rem(me - (k * SHOTS + s) + n, n)]

        summed = lax.fori_loop(0, slabs, slab_term, jnp.zeros((8, FX), F32))
        traces_out[s] = summed[:STEPS]

    total[...] = gr[shot + 1]
    for j in range(1, SHOTS):
        gr_copy(j).wait_recv()
        total[...] += grs[j]

    @pl.when((shot == SHOTS - 1) & has_high)
    def _():
        for s in range(SHOTS):
            low_copy(8 + s).wait_recv()
            total[...] += grs[8 + s]

    @pl.when((shot == 0) & has_low)
    def _():
        for s in range(SHOTS):
            high_copy(16 + s).wait_recv()
            total[...] += grs[16 + s]

    gradient_out[...] = total[...]

    store.wait()
    for part in range(PARTS):
        for side in range(2):

            @pl.when(sends[side])
            def _():
                lat_copy(side, part).wait_send()
                hid_copy(side, part).wait_send()

    for t in range(STEPS):
        for side in range(2):

            @pl.when(rim_sends[side])
            def _():
                rim_copy(side, t).wait_send()

    over_peers(lambda j: vel_copy(j).wait_send())
    over_peers(lambda j: rec_copy(j).wait_send())
    for j in range(1, SHOTS):
        gr_copy(j).wait_send()

    @pl.when(has_low)
    def _():
        low_copy(8 + shot).wait_send()

    @pl.when(has_high)
    def _():
        high_copy(16 + shot).wait_send()


def body(
    n,
    latent,
    conv1_weight,
    conv2_weight,
    head,
    p_prev,
    p_cur,
    adjoint,
    wavelet,
    sources,
    receivers,
):
    along_x, along_y, up_zy, up_zyt, up_x, up_xt = constants()
    vmem = pl.BlockSpec(memory_space=pltpu.VMEM)
    hbm = pl.BlockSpec(memory_space=pl.ANY)
    dma = pltpu.SemaphoreType.DMA
    final, traces, gradient = pl.pallas_call(
        functools.partial(kernel, n),
        out_shape=(
            jax.ShapeDtypeStruct((FPS, FY, FX), F32),
            jax.ShapeDtypeStruct((SHOTS, STEPS, 128), F32),
            jax.ShapeDtypeStruct((16, FX), F32),
        ),
        in_specs=[hbm] * 3 + [vmem] + [hbm] * 12,
        out_specs=(hbm, vmem, vmem),
        scratch_shapes=[
            pltpu.VMEM(conv1_weight.shape, BF16),
            pltpu.VMEM(conv2_weight.shape, BF16),
            pltpu.SMEM((STEPS, SHOTS), F32),
            pltpu.SMEM((3, SHOTS), jnp.int32),
            pltpu.VMEM((3, SHOTS, 128), jnp.int32),
            pltpu.VMEM(along_x.shape, BF16),
            pltpu.VMEM(along_y.shape, BF16),
            pltpu.VMEM(up_x.shape, BF16),
            pltpu.VMEM(up_xt.shape, BF16),
            pltpu.VMEM((FPS * FY, FX), F32),
            pltpu.VMEM((CH, 128), F32),
            pltpu.VMEM((3, CH, CELLS), BF16),
            pltpu.VMEM((3, CH, CELLS), BF16),
            pltpu.VMEM((9 * CH, 3 * CH), BF16),
            pltpu.VMEM((9 * CH, 3 * CH), BF16),
            pltpu.VMEM((9, CH, CELLS), F32),
            pltpu.VMEM((16, FX), BF16),
            pltpu.VMEM((n, 16, FX), BF16),
            pltpu.VMEM((2, FPS + 8, FY, FX), F32),
            pltpu.VMEM((STEPS, FPS, FY, FX), BF16),
            pltpu.VMEM(up_zy.shape, BF16),
            pltpu.VMEM(up_zyt.shape, BF16),
            pltpu.VMEM((FPS * FY, FX), F32),
            pltpu.VMEM((FPS * FY, FX), F32),
            pltpu.VMEM((2, STEPS, 4 * FY, FX), BF16),
            pltpu.VMEM((2, STEPS, 4 * FY, FX), BF16),
            pltpu.VMEM((FPS * FY, FX), BF16),
            pltpu.VMEM((8, FX), F32),
            pltpu.VMEM((n, 8, FX), F32),
            pltpu.VMEM((SHOTS + 2, 16, FX), F32),
            pltpu.VMEM((3 * SHOTS, 16, FX), F32),
            pltpu.VMEM((16, FX), F32),
            dma((16,)),
            dma((2, PARTS)),
            dma((2, PARTS)),
            dma((2, PARTS)),
            dma((2, PARTS)),
            dma((2, STEPS)),
            dma((2, STEPS)),
            dma((n,)),
            dma((n,)),
            dma((n,)),
            dma((n,)),
            dma((10,)),
            dma((3 * SHOTS,)),
        ],
        compiler_params=pltpu.CompilerParams(
            collective_id=0, has_side_effects=True, vmem_limit_bytes=VMEM_BYTES
        ),
    )(
        latent.reshape(CH, CELLS),
        conv1_weight,
        conv2_weight,
        head.reshape(1, CH),
        wavelet.T,
        sources.T,
        receivers.transpose(1, 0, 2),
        along_x,
        along_y,
        up_x,
        up_xt,
        p_prev[0],
        p_cur[0],
        adjoint[:, 0],
        up_zy,
        up_zyt,
    )
    return final[None], traces, gradient.reshape(1, CELLS)


def solution(mesh):
    in_specs = (
        P(None, ("groups", "slab"), None),
        P(),
        P(),
        P(),
        P(("groups", "slab"), None, None, None),
        P(("groups", "slab"), None, None, None),
        P(None, ("groups", "slab"), None, None, None),
        P("groups", None),
        P("groups", None),
        P("groups", None, None),
    )
    out_specs = (
        P(("groups", "slab"), None, None, None),
        P("groups", None, None),
        P(("groups", "slab"), None),
    )
    return jax.shard_map(
        functools.partial(body, mesh.shape["slab"]),
        mesh=mesh,
        in_specs=in_specs,
        out_specs=out_specs,
        check_vma=False,
    )
```
